32 devices in a mesh: trial: 2 (over x), tx: 4 (over y, core), ty: 4 (over z).
Axes of the slice: x: 2, y: 2, z: 4, core: 2. Of those that a mesh axis runs over, the one named last changes fastest.
Arguments:
- velocity: float32 [2, 64, 256, 128], P('trial', 'tx', 'ty'), may hold values from 1.5 to 4
- direction: float32 [2, 64, 256, 128], P('trial', 'tx', 'ty'), may hold values from -0.5 to 0.5
- wave_prev: float32 [2, 64, 256, 128], P('trial', 'tx', 'ty'), may hold values from -6 to 6
- wave_now: float32 [2, 64, 256, 128], P('trial', 'tx', 'ty'), may hold values from -5.5 to 5.5, as said below
- winner: int32 [1], replicated, may hold values from 0 to 2047
- step_lengths: float32 [2], replicated, may hold values from 0.05 to 0.5
- src_cell: int32 [1], replicated, may hold values from 0 to 2097151
- wavelet: float32 [8], replicated, may hold values from -6000 to 6000
- rec_cells: int32 [2048], replicated, may hold values from 0 to 2097151
- observed: float32 [8, 2048], replicated, may hold values from -6 to 6
Outputs:
- wave_final: float32 [2, 64, 256, 128], P('trial', 'tx', 'ty')
- misfit: float32 [2], P('trial')
The draws below stay inside these ranges and needn't reach their ends.
Inputs may be any that keep to these rules, and one draw needn't show every extreme that they name: `wave_now`: drawn as a normal field clipped to -5 to 5, possibly with a constant offset.
All inputs are finite; a program needn't handle non-finite values.
Results may differ from the reference program's by a relative error of at most 0.0001.
Values sent between devices are 32-bit elements; how exact they have to be, the bound alone decides.
A program may use at most 64 MiB of HBM per device.

```python
import math
import jax
import jax.numpy as jnp
from jax import lax

NZ = 128
ITERS = 8
NREC = 2048
TRIALS = 2
NX = 64
NY = 256


def draw_wave_now(key, part):
    values = jnp.clip(jax.random.normal(key, (TRIALS, NX, NY, NZ), jnp.float32), -5.0, 5.0)
    return values


def touch_ends(drawn, own_key, low, top_value):
    place = [jax.random.randint(jax.random.fold_in(own_key, axis), (), 0, length) for axis, length in enumerate(drawn.shape)]
    main_axis = drawn.shape.index(max(drawn.shape))
    next_to = place[:main_axis] + [(place[main_axis] + 1) % drawn.shape[main_axis]] + place[main_axis + 1:]
    return drawn.at[tuple(place)].set(low).at[tuple(next_to)].set(top_value)


def block_levels(own_key, dims, cuts, low, largest):
    def one(dim, parts):
        steps = jax.random.uniform(jax.random.fold_in(jax.random.fold_in(own_key, 6), dim), (parts,), jnp.float32, low / len(cuts), largest / len(cuts))
        return jnp.repeat(jnp.exp(steps), dims[dim] // parts).reshape((-1,) + (1,) * (len(dims) - dim - 1))

    gain = one(*cuts[0])
    for cut in cuts[1:]:
        gain = gain * one(*cut)
    return gain


def scatter_about(stream_key, extent, spread, reach, shards=(), kind=jnp.bfloat16):
    entries = spread * jax.random.normal(stream_key, extent, jnp.float32)
    if shards:
        entries = entries * block_levels(stream_key, extent, shards, -0.22, 0.18)
    return jnp.clip(entries, -reach, reach).astype(kind)


def setup_inputs(seed: int = 0) -> dict:
    key_of = jax.random.split(jax.random.key(seed), 11)
    velocity = jnp.clip(1.5 + 2.5 * jax.random.uniform(key_of[0], (TRIALS, NX, NY, NZ), jnp.float32) ** block_levels(key_of[0], (TRIALS, NX, NY, NZ), ((0, 2), (1, 4), (2, 4)), -0.2, 0.2), 1.5, 4.0)
    direction = jnp.clip(jax.random.uniform(key_of[1], (TRIALS, NX, NY, NZ), jnp.float32, -0.5, 0.5) * block_levels(key_of[1], (TRIALS, NX, NY, NZ), ((0, 2), (1, 4), (2, 4)), -0.4, 0.0), -0.5, 0.5)
    wave_prev = scatter_about(key_of[2], (TRIALS, NX, NY, NZ), 1.0, 6.0, ((0, 2), (1, 4), (2, 4)), jnp.float32)
    wave_now = draw_wave_now(jax.random.fold_in(key_of[10], 71), 0)
    winner = jax.random.randint(key_of[4], (1,), 0, TRIALS * 1024).astype(jnp.int32)
    step_lengths = jnp.clip(jnp.exp(jax.random.uniform(key_of[5], (TRIALS,), jnp.float32, math.log(0.05), math.log(0.5))), 0.05, 0.5)
    src_cell = jax.random.randint(key_of[6], (1,), 0, NX * NY * NZ).astype(jnp.int32)
    wavelet = scatter_about(key_of[7], (ITERS,), 1500.0, 6000.0, (), jnp.float32)
    rec_cells = touch_ends(jax.random.randint(key_of[8], (NREC,), 0, NX * NY * NZ), jax.random.fold_in(key_of[8], 1), 0, (NX * NY * NZ) - 1).astype(jnp.int32)
    observed = scatter_about(key_of[9], (ITERS, NREC), 1.0, 6.0, (), jnp.float32)
    return dict(velocity=velocity, direction=direction, wave_prev=wave_prev, wave_now=wave_now, winner=winner, step_lengths=step_lengths, src_cell=src_cell, wavelet=wavelet, rec_cells=rec_cells, observed=observed)


coef_mid = -2.5
coef_one = 4.0 / 3.0
coef_two = -1.0 / 12.0
dt_over_h = 0.1


def laplace(field):
    padded = jnp.pad(field, 2)
    centre = padded[2:-2, 2:-2, 2:-2]
    total = 3.0 * coef_mid * centre
    total = total + coef_one * (padded[3:-1, 2:-2, 2:-2] + padded[1:-3, 2:-2, 2:-2])
    total = total + coef_two * (padded[4:, 2:-2, 2:-2] + padded[:-4, 2:-2, 2:-2])
    total = total + coef_one * (padded[2:-2, 3:-1, 2:-2] + padded[2:-2, 1:-3, 2:-2])
    total = total + coef_two * (padded[2:-2, 4:, 2:-2] + padded[2:-2, :-4, 2:-2])
    total = total + coef_one * (padded[2:-2, 2:-2, 3:-1] + padded[2:-2, 2:-2, 1:-3])
    total = total + coef_two * (padded[2:-2, 2:-2, 4:] + padded[2:-2, 2:-2, :-4])
    return total


def reference(velocity, direction, wave_prev, wave_now, winner, step_lengths, src_cell, wavelet, rec_cells, observed):
    chosen = (winner[0] % TRIALS).astype(jnp.int32)
    accepted = lax.dynamic_index_in_dim(velocity, chosen, 0, keepdims=False)
    heading = lax.dynamic_index_in_dim(direction, chosen, 0, keepdims=False)
    source = jnp.zeros((NX * NY * NZ,), jnp.float32).at[src_cell[0]].set(1.0).reshape(NX, NY, NZ)

    def one_trial(items):
        alpha, prev, now = items
        speed = ((accepted + alpha * heading) * dt_over_h) ** 2
        total = jnp.float32(0.0)
        for step in range(ITERS):
            nxt = 2.0 * now - prev + speed * (laplace(now) + wavelet[step] * source)
            picked = jnp.take(nxt.reshape(-1), rec_cells)
            total = total + jnp.sum((picked - observed[step]) ** 2)
            prev, now = now, nxt
        return now, total / (ITERS * NREC)

    wave_final, misfit = lax.map(one_trial, (step_lengths, wave_prev, wave_now))
    return wave_final, misfit
```

```python
import functools

import jax
import jax.numpy as jnp
from jax import lax
from jax.experimental import pallas as pl
from jax.experimental.pallas import tpu as pltpu
from jax.sharding import PartitionSpec as P

MESH = pl.DeviceIdType.MESH
coef_mid = -2.5
coef_one = 4.0 / 3.0
coef_two = -1.0 / 12.0
dt_over_h = 0.1
HALO = 2
PAD = 8
CHUNK = 256


def from_root(block, axis, source):
    block = jnp.where(lax.axis_index(axis) == source, block, jnp.zeros_like(block))
    return lax.psum(block, axis)


def kernel(
    sizes,
    vel_ref,
    dir_ref,
    prev_ref,
    now_ref,
    winner_ref,
    steps_ref,
    src_ref,
    wavelet_ref,
    recrow_ref,
    recz_ref,
    obs_ref,
    out_ref,
    misfit_ref,
    field,
    speed,
    speed_out,
    speed_in,
    y_out,
    y_in,
    hot,
    lhs,
    acc,
    red,
    x_send,
    x_recv,
    y_send,
    y_recv,
    sp_send,
    sp_recv,
    red_send,
    red_recv,
):
    trials, tiles_x, tiles_y = sizes
    cells_x, cells_y, depth = now_ref.shape[1:]
    iters, nrec = obs_ref.shape
    exchange = trials == 2
    k = lax.axis_index("trial")
    ix = lax.axis_index("tx")
    iy = lax.axis_index("ty")
    inner_x = pl.ds(HALO, cells_x)
    inner_y = pl.ds(PAD, cells_y)

    for slot in range(2):
        for x in (0, 1, HALO + cells_x, HALO + cells_x + 1):
            field[slot, x] = jnp.zeros(field.shape[2:], jnp.float32)
        field[slot, inner_x, pl.ds(0, PAD)] = jnp.zeros((cells_x, PAD, depth), jnp.float32)
        field[slot, inner_x, pl.ds(PAD + cells_y, PAD)] = jnp.zeros(
            (cells_x, PAD, depth), jnp.float32
        )

    barrier = pltpu.get_barrier_semaphore()
    greeted = 0
    for d in range(1, tiles_x):
        pl.semaphore_signal(
            barrier, inc=1, device_id={"tx": lax.rem(ix + d, tiles_x)}, device_id_type=MESH
        )
        greeted += 1
    for d in range(1, tiles_y):
        pl.semaphore_signal(
            barrier, inc=1, device_id={"ty": lax.rem(iy + d, tiles_y)}, device_id_type=MESH
        )
        greeted += 1
    if exchange:
        pl.semaphore_signal(barrier, inc=1, device_id={"trial": 1 - k}, device_id_type=MESH)
        greeted += 1

    mine = steps_ref[k]
    if exchange:
        other = steps_ref[1 - k]

    def speeds(x, _):
        v = vel_ref[0, x]
        d = dir_ref[0, x]
        own = (v + mine * d) * dt_over_h
        speed[x] = own * own
        if exchange:
            far = (v + other * d) * dt_over_h
            speed_out[x] = far * far
        field[0, HALO + x, inner_y] = now_ref[0, x]
        field[1, HALO + x, inner_y] = prev_ref[0, x]
        return 0

    lax.fori_loop(0, cells_x, speeds, 0)
    if greeted:
        pl.semaphore_wait(barrier, greeted)

    def x_copy(slot, side):
        src = HALO if side == 0 else cells_x
        dst = HALO + cells_x if side == 0 else 0
        to = jnp.maximum(ix - 1, 0) if side == 0 else jnp.minimum(ix + 1, tiles_x - 1)
        return pltpu.make_async_remote_copy(
            src_ref=field.at[slot, pl.ds(src, HALO), inner_y],
            dst_ref=field.at[slot, pl.ds(dst, HALO), inner_y],
            send_sem=x_send.at[slot, side],
            recv_sem=x_recv.at[slot, side],
            device_id={"tx": to},
            device_id_type=MESH,
        )

    def y_copy(slot, side):
        to = jnp.maximum(iy - 1, 0) if side == 0 else jnp.minimum(iy + 1, tiles_y - 1)
        return pltpu.make_async_remote_copy(
            src_ref=y_out.at[slot, side],
            dst_ref=y_in.at[slot, side],
            send_sem=y_send.at[slot, side],
            recv_sem=y_recv.at[slot, side],
            device_id={"ty": to},
            device_id_type=MESH,
        )

    below_x, above_x = ix > 0, ix < tiles_x - 1
    below_y, above_y = iy > 0, iy < tiles_y - 1

    def send_faces(slot):
        @pl.when(below_x)
        def _():
            x_copy(slot, 0).start()

        @pl.when(above_x)
        def _():
            x_copy(slot, 1).start()

        for j in range(HALO):
            y_out[slot, 0, j] = field[slot, inner_x, PAD + j, :]
            y_out[slot, 1, j] = field[slot, inner_x, PAD + cells_y - HALO + j, :]

        @pl.when(below_y)
        def _():
            y_copy(slot, 0).start()

        @pl.when(above_y)
        def _():
            y_copy(slot, 1).start()

    def take_faces(slot):
        @pl.when(below_x)
        def _():
            x_copy(slot, 1).wait_recv()
            x_copy(slot, 0).wait_send()

        @pl.when(above_x)
        def _():
            x_copy(slot, 0).wait_recv()
            x_copy(slot, 1).wait_send()

        @pl.when(below_y)
        def _():
            y_copy(slot, 1).wait_recv()
            y_copy(slot, 0).wait_send()
            for j in range(HALO):
                field[slot, inner_x, PAD - HALO + j, :] = y_in[slot, 1, j]

        @pl.when(above_y)
        def _():
            y_copy(slot, 0).wait_recv()
            y_copy(slot, 1).wait_send()
            for j in range(HALO):
                field[slot, inner_x, PAD + cells_y + j, :] = y_in[slot, 0, j]

    send_faces(0)
    if exchange:
        speed_copy = pltpu.make_async_remote_copy(
            src_ref=speed_out,
            dst_ref=speed_in,
            send_sem=sp_send,
            recv_sem=sp_recv,
            device_id={"trial": 1 - k},
            device_id_type=MESH,
        )
        speed_copy.start()

    rows = cells_x * cells_y
    step_rows = 256 if rows % 256 == 0 else rows
    for c in range(nrec // CHUNK):
        at = recrow_ref[:, c * CHUNK : (c + 1) * CHUNK]

        def mark(b, _, c=c, at=at):
            row = lax.broadcasted_iota(jnp.int32, (step_rows, CHUNK), 0) + b * step_rows
            start = pl.multiple_of(b * step_rows, step_rows)
            hot[c, pl.ds(start, step_rows)] = jnp.where(row == at, 1.0, 0.0).astype(jnp.bfloat16)
            return 0

        lax.fori_loop(0, rows // step_rows, mark, 0)
    acc[...] = jnp.zeros_like(acc)

    whole_y = cells_y * tiles_y
    flat = src_ref[0]
    src_x = lax.div(flat, whole_y * depth) - ix * cells_x
    in_plane = lax.rem(flat, whole_y * depth)
    src_y = lax.div(in_plane, depth) - iy * cells_y
    src_yz = jnp.where(
        (src_y >= 0) & (src_y < cells_y), src_y * depth + lax.rem(in_plane, depth), -1
    )

    plane = (cells_y, depth)
    lane = lax.broadcasted_iota(jnp.int32, (1, depth), 1)
    up1 = jnp.where(lane >= 1, coef_one, 0.0).astype(jnp.float32)
    up2 = jnp.where(lane >= 2, coef_two, 0.0).astype(jnp.float32)
    dn1 = jnp.where(lane < depth - 1, coef_one, 0.0).astype(jnp.float32)
    dn2 = jnp.where(lane < depth - 2, coef_two, 0.0).astype(jnp.float32)

    if exchange:
        speed_copy.wait()
        who = jnp.full(plane, lax.rem(winner_ref[0], trials), jnp.int32)
        keep = who == k

        def choose(x, _):
            speed[x] = jnp.where(keep, speed[x], speed_in[x])
            return 0

        lax.fori_loop(0, cells_x, choose, 0)

    def step(t, _):
        slot = lax.rem(t, 2)
        late = 1 - slot
        take_faces(slot)
        amp = wavelet_ref[t]

        def advance(x, _):
            u = field[slot, x + HALO, inner_y]
            total = (3.0 * coef_mid) * u
            near = field[slot, x + 3, inner_y] + field[slot, x + 1, inner_y]
            far = field[slot, x + 4, inner_y] + field[slot, x, inner_y]
            near = near + (
                field[slot, x + HALO, pl.ds(PAD + 1, cells_y)]
                + field[slot, x + HALO, pl.ds(PAD - 1, cells_y)]
            )
            far = far + (
                field[slot, x + HALO, pl.ds(PAD + 2, cells_y)]
                + field[slot, x + HALO, pl.ds(PAD - 2, cells_y)]
            )
            total = total + coef_one * near + coef_two * far
            total = total + up1 * pltpu.roll(u, 1, 1) + dn1 * pltpu.roll(u, depth - 1, 1)
            total = total + up2 * pltpu.roll(u, 2, 1) + dn2 * pltpu.roll(u, depth - 2, 1)
            place = lax.broadcasted_iota(jnp.int32, plane, 0) * depth
            place = place + lax.broadcasted_iota(jnp.int32, plane, 1)
            here = jnp.where(src_x == x, src_yz, -1)
            total = total + jnp.where(place == here, amp, 0.0)
            prev = field[late, x + HALO, inner_y]
            field[late, x + HALO, inner_y] = 2.0 * u - prev + speed[x] * total
            return 0

        lax.fori_loop(0, cells_x, advance, 0)

        @pl.when(t < iters - 1)
        def _():
            send_faces(late)

        pair = max(1, 128 // cells_y)
        wide = pair * cells_y
        for p in range(cells_x // pair):
            block = field[late, pl.ds(HALO + p * pair, pair), inner_y]
            turned = block.reshape(wide, depth).T
            high = turned.astype(jnp.bfloat16)
            left = turned - high.astype(jnp.float32)
            middle = left.astype(jnp.bfloat16)
            low = (left - middle.astype(jnp.float32)).astype(jnp.bfloat16)
            lhs[0:depth, p * wide : (p + 1) * wide] = high
            lhs[depth : 2 * depth, p * wide : (p + 1) * wide] = middle
            lhs[2 * depth : 3 * depth, p * wide : (p + 1) * wide] = low
        zs = lax.broadcasted_iota(jnp.int32, (depth, CHUNK), 0)
        for c in range(nrec // CHUNK):
            got = jnp.dot(lhs[...], hot[c], preferred_element_type=jnp.float32)
            picked = got[:depth] + (got[depth : 2 * depth] + got[2 * depth :])
            cols = pl.ds(c * CHUNK, CHUNK)
            gap = picked - obs_ref[pl.ds(t, 1), cols]
            part = jnp.where(zs == recz_ref[:, cols], gap * gap, 0.0)
            part = part.reshape(depth // 8, 8, CHUNK).sum(axis=0)
            acc[...] += part[:, :128] + part[:, 128:]
        return 0

    lax.fori_loop(0, iters, step, 0)

    for phase, (axis, me, count) in enumerate((("tx", ix, tiles_x), ("ty", iy, tiles_y))):
        red[phase, 0] = acc[...]
        copies = []
        for d in range(1, count):
            copy = pltpu.make_async_remote_copy(
                src_ref=red.at[phase, 0],
                dst_ref=red.at[phase, d],
                send_sem=red_send.at[phase, d],
                recv_sem=red_recv.at[phase, d],
                device_id={axis: lax.rem(me + d, count)},
                device_id_type=MESH,
            )
            copy.start()
            copies.append(copy)
        if phase == 0:
            last = iters % 2
            out_ref[0] = field[last, inner_x, inner_y]
        for copy in copies:
            copy.wait()
        total = red[phase, 0]
        for d in range(1, count):
            total = total + red[phase, d]
        acc[...] = total
    share = jnp.sum(acc[...], axis=(0, 1), keepdims=True) * (1.0 / (iters * nrec))
    misfit_ref[...] = jnp.broadcast_to(share, misfit_ref.shape)


def local(
    sizes,
    velocity,
    direction,
    wave_prev,
    wave_now,
    winner,
    step_lengths,
    src_cell,
    wavelet,
    rec_cells,
    observed,
):
    trials, tiles_x, tiles_y = sizes
    cells_x, cells_y, depth = velocity.shape[1:]
    iters, nrec = observed.shape
    if trials != 2:
        root = winner[0] % trials
        velocity = from_root(velocity, "trial", root)
        direction = from_root(direction, "trial", root)
    plane = cells_y * tiles_y * depth
    rec_x = rec_cells // plane - lax.axis_index("tx") * cells_x
    rec_y = rec_cells % plane // depth - lax.axis_index("ty") * cells_y
    inside = (rec_x >= 0) & (rec_x < cells_x) & (rec_y >= 0) & (rec_y < cells_y)
    rec_row = jnp.where(inside, rec_x * cells_y + rec_y, -1).reshape(1, nrec)
    rec_z = jnp.where(inside, rec_cells % depth, -1).reshape(1, nrec)
    vmem = pl.BlockSpec(memory_space=pltpu.VMEM)
    smem = pl.BlockSpec(memory_space=pltpu.SMEM)
    block = (cells_x, cells_y, depth)
    faces = (2, 2, HALO, cells_x, depth)
    most = max(tiles_x, tiles_y)
    out, misfit = pl.pallas_call(
        functools.partial(kernel, sizes),
        out_shape=(
            jax.ShapeDtypeStruct((1,) + block, jnp.float32),
            jax.ShapeDtypeStruct((1, 128), jnp.float32),
        ),
        in_specs=[vmem] * 4 + [smem] * 4 + [vmem] * 3,
        out_specs=(vmem, vmem),
        scratch_shapes=[
            pltpu.VMEM((2, cells_x + 2 * HALO, cells_y + 2 * PAD, depth), jnp.float32),
            pltpu.VMEM(block, jnp.float32),
            pltpu.VMEM(block, jnp.float32),
            pltpu.VMEM(block, jnp.float32),
            pltpu.VMEM(faces, jnp.float32),
            pltpu.VMEM(faces, jnp.float32),
            pltpu.VMEM((nrec // CHUNK, cells_x * cells_y, CHUNK), jnp.bfloat16),
            pltpu.VMEM((3 * depth, cells_x * cells_y), jnp.bfloat16),
            pltpu.VMEM((8, 128), jnp.float32),
            pltpu.VMEM((2, most, 8, 128), jnp.float32),
            pltpu.SemaphoreType.DMA((2, 2)),
            pltpu.SemaphoreType.DMA((2, 2)),
            pltpu.SemaphoreType.DMA((2, 2)),
            pltpu.SemaphoreType.DMA((2, 2)),
            pltpu.SemaphoreType.DMA,
            pltpu.SemaphoreType.DMA,
            pltpu.SemaphoreType.DMA((2, most)),
            pltpu.SemaphoreType.DMA((2, most)),
        ],
        compiler_params=pltpu.CompilerParams(
            collective_id=0, has_side_effects=True, vmem_limit_bytes=40 * 1024 * 1024
        ),
    )(
        velocity,
        direction,
        wave_prev,
        wave_now,
        winner,
        step_lengths,
        src_cell,
        wavelet,
        rec_row,
        rec_z,
        observed,
    )
    return out, misfit[0, :1]


def solution(mesh):
    sizes = tuple(mesh.shape[axis] for axis in ("trial", "tx", "ty"))
    spread = P("trial", "tx", "ty", None)
    return jax.shard_map(
        functools.partial(local, sizes),
        mesh=mesh,
        in_specs=(spread,) * 4 + (P(),) * 6,
        out_specs=(spread, P("trial")),
        check_vma=False,
    )
```

```python
import functools

import jax
import jax.numpy as jnp
from jax import lax
from jax.experimental import pallas as pl
from jax.experimental.pallas import tpu as pltpu
from jax.sharding import PartitionSpec as P

MESH = pl.DeviceIdType.MESH
coef_mid = -2.5
coef_one = 4.0 / 3.0
coef_two = -1.0 / 12.0
dt_over_h = 0.1
HALO = 2
PAD = 8
CHUNK = 256
PLANES = 4
PARTS = 2


def quotient(value, by):
    if by & (by - 1) == 0:
        return lax.shift_right_logical(value, jnp.full_like(value, by.bit_length() - 1))
    return lax.div(value, jnp.full_like(value, by))


def parts(value):
    pieces = []
    for _ in range(PARTS):
        piece = value.astype(jnp.bfloat16)
        pieces.append(piece)
        value = value - piece.astype(jnp.float32)
    return pieces


def from_root(block, axis, source):
    block = jnp.where(lax.axis_index(axis) == source, block, jnp.zeros_like(block))
    return lax.psum(block, axis)


def kernel(
    sizes,
    vel_ref,
    dir_ref,
    prev_ref,
    now_ref,
    winner_ref,
    steps_ref,
    src_ref,
    wavelet_ref,
    rec_hbm,
    obs_hbm,
    out_ref,
    misfit_ref,
    field,
    rec_z,
    speed,
    speed_out,
    speed_in,
    y_out,
    y_in,
    hot,
    lhs,
    acc,
    red,
    x_send,
    x_recv,
    y_send,
    y_recv,
    sp_send,
    sp_recv,
    red_send,
    red_recv,
    vel,
    head,
    in_sem,
    wave_sem,
    out_sem,
    rec_ref,
    obs_ref,
    band,
    data_sem,
):
    trials, tiles_x, tiles_y = sizes
    cells_x, cells_y, depth = now_ref.shape[1:]
    groups = cells_x // PLANES
    iters, nrec = obs_hbm.shape
    exchange = trials == 2
    k = lax.axis_index("trial")
    ix = lax.axis_index("tx")
    iy = lax.axis_index("ty")
    inner_x = pl.ds(HALO, cells_x)
    inner_y = pl.ds(PAD, cells_y)

    loads = []
    for g in range(groups):
        some = pl.ds(g * PLANES, PLANES)
        pair = (
            pltpu.make_async_copy(vel_ref.at[0, some], vel.at[some], in_sem.at[0, g]),
            pltpu.make_async_copy(dir_ref.at[0, some], head.at[some], in_sem.at[1, g]),
        )
        for load in pair:
            load.start()
        loads.append(pair)
    waves = (
        pltpu.make_async_copy(now_ref.at[0], field.at[0, inner_x, inner_y], wave_sem.at[0]),
        pltpu.make_async_copy(prev_ref.at[0], field.at[1, inner_x, inner_y], wave_sem.at[1]),
    )
    data = (
        pltpu.make_async_copy(rec_hbm, rec_ref, data_sem.at[0]),
        pltpu.make_async_copy(obs_hbm, obs_ref, data_sem.at[1]),
    )
    for load in waves + data:
        load.start()

    for slot in range(2):
        for x in (0, 1, HALO + cells_x, HALO + cells_x + 1):
            field[slot, x] = jnp.zeros(field.shape[2:], jnp.float32)
        field[slot, inner_x, pl.ds(0, PAD)] = jnp.zeros((cells_x, PAD, depth), jnp.float32)
        field[slot, inner_x, pl.ds(PAD + cells_y, PAD)] = jnp.zeros(
            (cells_x, PAD, depth), jnp.float32
        )

    peers = [
        {"tx": lax.rem(ix + dx, tiles_x), "ty": lax.rem(iy + dy, tiles_y)}
        for dx in range(tiles_x)
        for dy in range(tiles_y)
    ]
    greet = peers[1:] + ([{"trial": 1 - k}] if exchange else [])
    barrier = pltpu.get_barrier_semaphore()
    for peer in greet:
        pl.semaphore_signal(barrier, inc=1, device_id=peer, device_id_type=MESH)

    mine = steps_ref[k]
    if exchange:
        other = steps_ref[1 - k]

    def speed_copy(g):
        some = pl.ds(g * PLANES, PLANES)
        return pltpu.make_async_remote_copy(
            src_ref=speed_out.at[some],
            dst_ref=speed_in.at[some],
            send_sem=sp_send.at[g],
            recv_sem=sp_recv.at[g],
            device_id={"trial": 1 - k},
            device_id_type=MESH,
        )

    for g in range(groups):
        for load in loads[g]:
            load.wait()
        some = pl.ds(g * PLANES, PLANES)
        v, d = vel[some], head[some]
        if exchange:
            far = (v + other * d) * dt_over_h
            speed_out[some] = far * far
        own = (v + mine * d) * dt_over_h
        speed[some] = own * own
        if g == 0 and greet:
            pl.semaphore_wait(barrier, len(greet))
        if exchange:
            speed_copy(g).start()
    for load in waves:
        load.wait()

    def x_copy(slot, side):
        src = HALO if side == 0 else cells_x
        dst = HALO + cells_x if side == 0 else 0
        to = jnp.maximum(ix - 1, 0) if side == 0 else jnp.minimum(ix + 1, tiles_x - 1)
        return pltpu.make_async_remote_copy(
            src_ref=field.at[slot, pl.ds(src, HALO), inner_y],
            dst_ref=field.at[slot, pl.ds(dst, HALO), inner_y],
            send_sem=x_send.at[slot, side],
            recv_sem=x_recv.at[slot, side],
            device_id={"tx": to},
            device_id_type=MESH,
        )

    def y_copy(slot, side):
        to = jnp.maximum(iy - 1, 0) if side == 0 else jnp.minimum(iy + 1, tiles_y - 1)
        return pltpu.make_async_remote_copy(
            src_ref=y_out.at[slot, side],
            dst_ref=y_in.at[slot, side],
            send_sem=y_send.at[slot, side],
            recv_sem=y_recv.at[slot, side],
            device_id={"ty": to},
            device_id_type=MESH,
        )

    below_x, above_x = ix > 0, ix < tiles_x - 1
    below_y, above_y = iy > 0, iy < tiles_y - 1

    def send_x(slot):
        @pl.when(below_x)
        def _():
            x_copy(slot, 0).start()

        @pl.when(above_x)
        def _():
            x_copy(slot, 1).start()

    def send_y(slot):
        for j in range(HALO):
            y_out[slot, 0, j] = field[slot, inner_x, PAD + j, :]
            y_out[slot, 1, j] = field[slot, inner_x, PAD + cells_y - HALO + j, :]

        @pl.when(below_y)
        def _():
            y_copy(slot, 0).start()

        @pl.when(above_y)
        def _():
            y_copy(slot, 1).start()

    def take_faces(slot):
        @pl.when(below_x)
        def _():
            x_copy(slot, 1).wait_recv()
            x_copy(slot, 0).wait_send()

        @pl.when(above_x)
        def _():
            x_copy(slot, 0).wait_recv()
            x_copy(slot, 1).wait_send()

        @pl.when(below_y)
        def _():
            y_copy(slot, 1).wait_recv()
            y_copy(slot, 0).wait_send()
            for j in range(HALO):
                field[slot, inner_x, PAD - HALO + j, :] = y_in[slot, 1, j]

        @pl.when(above_y)
        def _():
            y_copy(slot, 0).wait_recv()
            y_copy(slot, 1).wait_send()
            for j in range(HALO):
                field[slot, inner_x, PAD + cells_y + j, :] = y_in[slot, 0, j]

    send_x(0)
    send_y(0)
    rows = cells_x * cells_y
    step_rows = 256 if rows % 256 == 0 else rows
    whole_y = cells_y * tiles_y
    for load in data:
        load.wait()
    cell = rec_ref[...]
    rec_x = quotient(cell, whole_y * depth)
    rec_y = quotient(cell - rec_x * (whole_y * depth), depth)
    z = cell - (rec_x * whole_y + rec_y) * depth
    rec_x = rec_x - ix * cells_x
    rec_y = rec_y - iy * cells_y
    inside = (rec_x >= 0) & (rec_x < cells_x) & (rec_y >= 0) & (rec_y < cells_y)
    rec_row = jnp.where(inside, rec_x * cells_y + rec_y, -1)
    rec_z[...] = jnp.where(inside, z, -1)
    for c in range(nrec // CHUNK):
        at = rec_row[:, c * CHUNK : (c + 1) * CHUNK]

        def mark(b, _, c=c, at=at):
            row = lax.broadcasted_iota(jnp.int32, (step_rows, CHUNK), 0) + b * step_rows
            start = pl.multiple_of(b * step_rows, step_rows)
            hot[c, pl.ds(start, step_rows)] = jnp.where(row == at, 1.0, 0.0).astype(jnp.bfloat16)
            return 0

        lax.fori_loop(0, rows // step_rows, mark, 0)
    acc[...] = jnp.zeros_like(acc)

    flat = src_ref[0]
    src_x = lax.div(flat, whole_y * depth) - ix * cells_x
    in_plane = lax.rem(flat, whole_y * depth)
    src_y = lax.div(in_plane, depth) - iy * cells_y
    src_yz = jnp.where(
        (src_y >= 0) & (src_y < cells_y), src_y * depth + lax.rem(in_plane, depth), -1
    )

    plane = (cells_y, depth)
    place = lax.broadcasted_iota(jnp.int32, plane, 0) * depth
    place = place + lax.broadcasted_iota(jnp.int32, plane, 1)
    source = lax.broadcasted_iota(jnp.int32, (depth, depth), 0)
    target = lax.broadcasted_iota(jnp.int32, (depth, depth), 1)
    apart = jnp.abs(source - target)
    for reach in (1, 2):
        ones = jnp.where(apart == reach, 1.0, 0.0).astype(jnp.bfloat16)
        for part in range(PARTS):
            band[part * depth : (part + 1) * depth, (reach - 1) * depth : reach * depth] = ones

    who = jnp.full(plane, lax.rem(winner_ref[0], trials), jnp.int32)
    keep = who == k
    result = pltpu.make_async_copy(
        field.at[iters % 2, inner_x, inner_y], out_ref.at[0], out_sem
    )

    def step(t, _):
        slot = lax.rem(t, 2)
        late = 1 - slot
        take_faces(slot)
        amp = wavelet_ref[t]

        def advance(x, near_z, far_z):
            u = field[slot, x + HALO, inner_y]
            total = (3.0 * coef_mid) * u
            near = field[slot, x + 3, inner_y] + field[slot, x + 1, inner_y]
            far = field[slot, x + 4, inner_y] + field[slot, x, inner_y]
            near = near + (
                field[slot, x + HALO, pl.ds(PAD + 1, cells_y)]
                + field[slot, x + HALO, pl.ds(PAD - 1, cells_y)]
            )
            far = far + (
                field[slot, x + HALO, pl.ds(PAD + 2, cells_y)]
                + field[slot, x + HALO, pl.ds(PAD - 2, cells_y)]
            )
            total = total + coef_one * (near + near_z) + coef_two * (far + far_z)
            here = jnp.where(src_x == x, src_yz, -1)
            total = total + jnp.where(place == here, amp, 0.0)
            prev = field[late, x + HALO, inner_y]
            field[late, x + HALO, inner_y] = 2.0 * u - prev + speed[x] * total

        def advance_some(g, _):
            if exchange:

                @pl.when(t == 0)
                def _():
                    speed_copy(g).wait()
                    for i in range(PLANES):
                        x = g * PLANES + i
                        speed[x] = jnp.where(keep, speed[x], speed_in[x])

            some = field[slot, pl.ds(HALO + g * PLANES, PLANES), inner_y]
            along = jnp.dot(
                jnp.concatenate(parts(some.reshape(PLANES * cells_y, depth)), axis=1),
                band[...],
                preferred_element_type=jnp.float32,
            )
            for i in range(PLANES):
                lines = along[i * cells_y : (i + 1) * cells_y]
                advance(g * PLANES + i, lines[:, :depth], lines[:, depth:])

        for g in sorted({0, groups - 1}):
            advance_some(g, 0)

        @pl.when(t < iters - 1)
        def _():
            send_x(late)

        for g in range(1, groups - 1):
            advance_some(g, 0)

        @pl.when(t < iters - 1)
        def _():
            send_y(late)

        @pl.when(t == iters - 1)
        def _():
            result.start()

        pair = max(1, 128 // cells_y)
        wide = pair * cells_y
        for p in range(cells_x // pair):
            block = field[late, pl.ds(HALO + p * pair, pair), inner_y]
            turned = block.reshape(wide, depth).T
            for part, piece in enumerate(parts(turned)):
                lhs[part * depth : (part + 1) * depth, p * wide : (p + 1) * wide] = piece
        zs = lax.broadcasted_iota(jnp.int32, (depth, CHUNK), 0)
        for c in range(nrec // CHUNK):
            got = jnp.dot(lhs[...], hot[c], preferred_element_type=jnp.float32)
            picked = got[:depth]
            for part in range(1, PARTS):
                picked = picked + got[part * depth : (part + 1) * depth]
            cols = pl.ds(c * CHUNK, CHUNK)
            gap = picked - obs_ref[pl.ds(t, 1), cols]
            part = jnp.where(zs == rec_z[:, cols], gap * gap, 0.0)
            part = part.reshape(depth // 8, 8, CHUNK).sum(axis=0)
            acc[...] += part[:, :128] + part[:, 128:]
        return 0

    lax.fori_loop(0, iters, step, 0)

    copies = []
    for d in range(1, len(peers)):
        copy = pltpu.make_async_remote_copy(
            src_ref=acc,
            dst_ref=red.at[d],
            send_sem=red_send.at[d],
            recv_sem=red_recv.at[d],
            device_id=peers[d],
            device_id_type=MESH,
        )
        copy.start()
        copies.append(copy)
    total = acc[...]
    for d, copy in enumerate(copies, 1):
        copy.wait()
        total = total + red[d]
    result.wait()
    share = jnp.sum(total, axis=(0, 1), keepdims=True) * (1.0 / (iters * nrec))
    misfit_ref[...] = jnp.broadcast_to(share, misfit_ref.shape)


def local(
    sizes,
    velocity,
    direction,
    wave_prev,
    wave_now,
    winner,
    step_lengths,
    src_cell,
    wavelet,
    rec_cells,
    observed,
):
    trials, tiles_x, tiles_y = sizes
    cells_x, cells_y, depth = velocity.shape[1:]
    iters, nrec = observed.shape
    if trials != 2:
        root = winner[0] % trials
        velocity = from_root(velocity, "trial", root)
        direction = from_root(direction, "trial", root)
    vmem = pl.BlockSpec(memory_space=pltpu.VMEM)
    smem = pl.BlockSpec(memory_space=pltpu.SMEM)
    block = (cells_x, cells_y, depth)
    faces = (2, 2, HALO, cells_x, depth)
    tiles = tiles_x * tiles_y
    groups = cells_x // PLANES
    whole = pl.BlockSpec(memory_space=pltpu.HBM)
    out, misfit = pl.pallas_call(
        functools.partial(kernel, sizes),
        out_shape=(
            jax.ShapeDtypeStruct((1,) + block, jnp.float32),
            jax.ShapeDtypeStruct((1, 128), jnp.float32),
        ),
        in_specs=[whole] * 4 + [smem] * 4 + [whole] * 2,
        out_specs=(whole, vmem),
        scratch_shapes=[
            pltpu.VMEM((2, cells_x + 2 * HALO, cells_y + 2 * PAD, depth), jnp.float32),
            pltpu.VMEM((1, nrec), jnp.int32),
            pltpu.VMEM(block, jnp.float32),
            pltpu.VMEM(block, jnp.float32),
            pltpu.VMEM(block, jnp.float32),
            pltpu.VMEM(faces, jnp.float32),
            pltpu.VMEM(faces, jnp.float32),
            pltpu.VMEM((nrec // CHUNK, cells_x * cells_y, CHUNK), jnp.bfloat16),
            pltpu.VMEM((PARTS * depth, cells_x * cells_y), jnp.bfloat16),
            pltpu.VMEM((8, 128), jnp.float32),
            pltpu.VMEM((tiles, 8, 128), jnp.float32),
            pltpu.SemaphoreType.DMA((2, 2)),
            pltpu.SemaphoreType.DMA((2, 2)),
            pltpu.SemaphoreType.DMA((2, 2)),
            pltpu.SemaphoreType.DMA((2, 2)),
            pltpu.SemaphoreType.DMA((groups,)),
            pltpu.SemaphoreType.DMA((groups,)),
            pltpu.SemaphoreType.DMA((tiles,)),
            pltpu.SemaphoreType.DMA((tiles,)),
            pltpu.VMEM(block, jnp.float32),
            pltpu.VMEM(block, jnp.float32),
            pltpu.SemaphoreType.DMA((2, groups)),
            pltpu.SemaphoreType.DMA((2,)),
            pltpu.SemaphoreType.DMA,
            pltpu.VMEM((1, nrec), jnp.int32),
            pltpu.VMEM((iters, nrec), jnp.float32),
            pltpu.VMEM((PARTS * depth, 2 * depth), jnp.bfloat16),
            pltpu.SemaphoreType.DMA((2,)),
        ],
        compiler_params=pltpu.CompilerParams(
            collective_id=0, has_side_effects=True, vmem_limit_bytes=62 * 1024 * 1024
        ),
    )(
        velocity,
        direction,
        wave_prev,
        wave_now,
        winner,
        step_lengths,
        src_cell,
        wavelet,
        rec_cells.reshape(1, nrec),
        observed,
    )
    return out, misfit[0, :1]


def solution(mesh):
    sizes = tuple(mesh.shape[axis] for axis in ("trial", "tx", "ty"))
    spread = P("trial", "tx", "ty", None)
    return jax.shard_map(
        functools.partial(local, sizes),
        mesh=mesh,
        in_specs=(spread,) * 4 + (P(),) * 6,
        out_specs=(spread, P("trial")),
        check_vma=False,
    )
```

```python
import functools

import jax
import jax.numpy as jnp
from jax import lax
from jax.experimental import pallas as pl
from jax.experimental.pallas import tpu as pltpu
from jax.sharding import PartitionSpec as P

MESH = pl.DeviceIdType.MESH
coef_mid = -2.5
coef_one = 4.0 / 3.0
coef_two = -1.0 / 12.0
dt_over_h = 0.1
HALO = 2
PAD = 8
CHUNK = 256
PLANES = 4
PARTS = 2


def quotient(value, by):
    if by & (by - 1) == 0:
        return lax.shift_right_logical(value, jnp.full_like(value, by.bit_length() - 1))
    return lax.div(value, jnp.full_like(value, by))


def parts(value):
    pieces = []
    for _ in range(PARTS):
        piece = value.astype(jnp.bfloat16)
        pieces.append(piece)
        value = value - piece.astype(jnp.float32)
    return pieces


def from_root(block, axis, source):
    block = jnp.where(lax.axis_index(axis) == source, block, jnp.zeros_like(block))
    return lax.psum(block, axis)


def kernel(
    sizes,
    vel_ref,
    dir_ref,
    prev_ref,
    now_ref,
    winner_ref,
    steps_ref,
    src_ref,
    wavelet_ref,
    rec_hbm,
    obs_hbm,
    out_ref,
    misfit_ref,
    field,
    rec_z,
    speed,
    speed_out,
    speed_in,
    y_out,
    y_in,
    hot,
    lhs,
    acc,
    red,
    x_send,
    x_recv,
    y_send,
    y_recv,
    sp_send,
    sp_recv,
    red_send,
    red_recv,
    vel,
    head,
    in_sem,
    wave_sem,
    out_sem,
    rec_ref,
    obs_ref,
    band,
    data_sem,
):
    trials, tiles_x, tiles_y = sizes
    cells_x, cells_y, depth = now_ref.shape[1:]
    groups = cells_x // PLANES
    iters, nrec = obs_hbm.shape
    exchange = trials == 2
    k = lax.axis_index("trial")
    ix = lax.axis_index("tx")
    iy = lax.axis_index("ty")
    inner_x = pl.ds(HALO, cells_x)
    inner_y = pl.ds(PAD, cells_y)

    loads = []
    for g in range(groups):
        some = pl.ds(g * PLANES, PLANES)
        pair = (
            pltpu.make_async_copy(vel_ref.at[0, some], vel.at[some], in_sem.at[0, g]),
            pltpu.make_async_copy(dir_ref.at[0, some], head.at[some], in_sem.at[1, g]),
        )
        for load in pair:
            load.start()
        loads.append(pair)
    waves = (
        pltpu.make_async_copy(now_ref.at[0], field.at[0, inner_x, inner_y], wave_sem.at[0]),
        pltpu.make_async_copy(prev_ref.at[0], field.at[1, inner_x, inner_y], wave_sem.at[1]),
    )
    data = (
        pltpu.make_async_copy(rec_hbm, rec_ref, data_sem.at[0]),
        pltpu.make_async_copy(obs_hbm, obs_ref, data_sem.at[1]),
    )
    for load in waves + data:
        load.start()

    for slot in range(2):
        for x in (0, 1, HALO + cells_x, HALO + cells_x + 1):
            field[slot, x] = jnp.zeros(field.shape[2:], jnp.float32)
        field[slot, inner_x, pl.ds(0, PAD)] = jnp.zeros((cells_x, PAD, depth), jnp.float32)
        field[slot, inner_x, pl.ds(PAD + cells_y, PAD)] = jnp.zeros(
            (cells_x, PAD, depth), jnp.float32
        )

    peers = [
        {"tx": lax.rem(ix + dx, tiles_x), "ty": lax.rem(iy + dy, tiles_y)}
        for dx in range(tiles_x)
        for dy in range(tiles_y)
    ]
    greet = peers[1:] + ([{"trial": 1 - k}] if exchange else [])
    barrier = pltpu.get_barrier_semaphore()
    for peer in greet:
        pl.semaphore_signal(barrier, inc=1, device_id=peer, device_id_type=MESH)

    mine = steps_ref[k]
    if exchange:
        other = steps_ref[1 - k]

    def speed_copy(g):
        some = pl.ds(g * PLANES, PLANES)
        return pltpu.make_async_remote_copy(
            src_ref=speed_out.at[some],
            dst_ref=speed_in.at[some],
            send_sem=sp_send.at[g],
            recv_sem=sp_recv.at[g],
            device_id={"trial": 1 - k},
            device_id_type=MESH,
        )

    for g in range(groups):
        for load in loads[g]:
            load.wait()
        some = pl.ds(g * PLANES, PLANES)
        v, d = vel[some], head[some]
        if exchange:
            far = (v + other * d) * dt_over_h
            speed_out[some] = far * far
        own = (v + mine * d) * dt_over_h
        speed[some] = own * own
        if g == 0 and greet:
            pl.semaphore_wait(barrier, len(greet))
        if exchange:
            speed_copy(g).start()
    for load in waves:
        load.wait()

    def x_copy(slot, side):
        src = HALO if side == 0 else cells_x
        dst = HALO + cells_x if side == 0 else 0
        to = jnp.maximum(ix - 1, 0) if side == 0 else jnp.minimum(ix + 1, tiles_x - 1)
        return pltpu.make_async_remote_copy(
            src_ref=field.at[slot, pl.ds(src, HALO), inner_y],
            dst_ref=field.at[slot, pl.ds(dst, HALO), inner_y],
            send_sem=x_send.at[slot, side],
            recv_sem=x_recv.at[slot, side],
            device_id={"tx": to},
            device_id_type=MESH,
        )

    def y_copy(slot, side):
        to = jnp.maximum(iy - 1, 0) if side == 0 else jnp.minimum(iy + 1, tiles_y - 1)
        return pltpu.make_async_remote_copy(
            src_ref=y_out.at[slot, side],
            dst_ref=y_in.at[slot, side],
            send_sem=y_send.at[slot, side],
            recv_sem=y_recv.at[slot, side],
            device_id={"ty": to},
            device_id_type=MESH,
        )

    below_x, above_x = ix > 0, ix < tiles_x - 1
    below_y, above_y = iy > 0, iy < tiles_y - 1

    def send_x(slot):
        @pl.when(below_x)
        def _():
            x_copy(slot, 0).start()

        @pl.when(above_x)
        def _():
            x_copy(slot, 1).start()

    def send_y(slot):
        for j in range(HALO):
            y_out[slot, 0, j] = field[slot, inner_x, PAD + j, :]
            y_out[slot, 1, j] = field[slot, inner_x, PAD + cells_y - HALO + j, :]

        @pl.when(below_y)
        def _():
            y_copy(slot, 0).start()

        @pl.when(above_y)
        def _():
            y_copy(slot, 1).start()

    def take_faces(slot):
        @pl.when(below_x)
        def _():
            x_copy(slot, 1).wait_recv()
            x_copy(slot, 0).wait_send()

        @pl.when(above_x)
        def _():
            x_copy(slot, 0).wait_recv()
            x_copy(slot, 1).wait_send()

        @pl.when(below_y)
        def _():
            y_copy(slot, 1).wait_recv()
            y_copy(slot, 0).wait_send()
            for j in range(HALO):
                field[slot, inner_x, PAD - HALO + j, :] = y_in[slot, 1, j]

        @pl.when(above_y)
        def _():
            y_copy(slot, 0).wait_recv()
            y_copy(slot, 1).wait_send()
            for j in range(HALO):
                field[slot, inner_x, PAD + cells_y + j, :] = y_in[slot, 0, j]

    send_x(0)
    send_y(0)
    rows = cells_x * cells_y
    step_rows = 256 if rows % 256 == 0 else rows
    whole_y = cells_y * tiles_y
    for load in data:
        load.wait()
    cell = rec_ref[...]
    rec_x = quotient(cell, whole_y * depth)
    rec_y = quotient(cell - rec_x * (whole_y * depth), depth)
    z = cell - (rec_x * whole_y + rec_y) * depth
    rec_x = rec_x - ix * cells_x
    rec_y = rec_y - iy * cells_y
    inside = (rec_x >= 0) & (rec_x < cells_x) & (rec_y >= 0) & (rec_y < cells_y)
    rec_row = jnp.where(inside, rec_x * cells_y + rec_y, -1)
    rec_z[...] = jnp.where(inside, z, -1)
    for c in range(nrec // CHUNK):
        at = rec_row[:, c * CHUNK : (c + 1) * CHUNK]

        def mark(b, _, c=c, at=at):
            row = lax.broadcasted_iota(jnp.int32, (step_rows, CHUNK), 0) + b * step_rows
            start = pl.multiple_of(b * step_rows, step_rows)
            hot[c, pl.ds(start, step_rows)] = jnp.where(row == at, 1.0, 0.0).astype(jnp.bfloat16)
            return 0

        lax.fori_loop(0, rows // step_rows, mark, 0)
    acc[...] = jnp.zeros_like(acc)

    flat = src_ref[0]
    src_x = lax.div(flat, whole_y * depth) - ix * cells_x
    in_plane = lax.rem(flat, whole_y * depth)
    src_y = lax.div(in_plane, depth) - iy * cells_y
    src_yz = jnp.where(
        (src_y >= 0) & (src_y < cells_y), src_y * depth + lax.rem(in_plane, depth), -1
    )

    plane = (cells_y, depth)
    place = lax.broadcasted_iota(jnp.int32, plane, 0) * depth
    place = place + lax.broadcasted_iota(jnp.int32, plane, 1)
    source = lax.broadcasted_iota(jnp.int32, (depth, depth), 0)
    target = lax.broadcasted_iota(jnp.int32, (depth, depth), 1)
    apart = jnp.abs(source - target)
    for reach in (1, 2):
        ones = jnp.where(apart == reach, 1.0, 0.0).astype(jnp.bfloat16)
        for part in range(PARTS):
            band[part * depth : (part + 1) * depth, (reach - 1) * depth : reach * depth] = ones

    who = jnp.full(plane, lax.rem(winner_ref[0], trials), jnp.int32)
    keep = who == k
    result = pltpu.make_async_copy(
        field.at[iters % 2, inner_x, inner_y], out_ref.at[0], out_sem
    )

    def step(t, _):
        slot = lax.rem(t, 2)
        late = 1 - slot
        take_faces(slot)
        amp = wavelet_ref[t]

        def advance(x, row, count, near_z, far_z):
            part_y = pl.ds(PAD + row, count)
            u = field[slot, x + HALO, part_y]
            total = (3.0 * coef_mid) * u
            near = field[slot, x + 3, part_y] + field[slot, x + 1, part_y]
            far = field[slot, x + 4, part_y] + field[slot, x, part_y]
            near = near + (
                field[slot, x + HALO, pl.ds(PAD + row + 1, count)]
                + field[slot, x + HALO, pl.ds(PAD + row - 1, count)]
            )
            far = far + (
                field[slot, x + HALO, pl.ds(PAD + row + 2, count)]
                + field[slot, x + HALO, pl.ds(PAD + row - 2, count)]
            )
            total = total + coef_one * (near + near_z) + coef_two * (far + far_z)
            here = jnp.where(src_x == x, src_yz, -1)
            total = total + jnp.where(place[row : row + count] == here, amp, 0.0)
            prev = field[late, x + HALO, part_y]
            field[late, x + HALO, part_y] = 2.0 * u - prev + speed[x, pl.ds(row, count)] * total

        def advance_some(first, planes, row, count):
            some = field[slot, pl.ds(HALO + first, planes), pl.ds(PAD + row, count)]
            along = jnp.dot(
                jnp.concatenate(parts(some.reshape(planes * count, depth)), axis=1),
                band[...],
                preferred_element_type=jnp.float32,
            )
            for i in range(planes):
                lines = along[i * count : (i + 1) * count]
                advance(first + i, row, count, lines[:, :depth], lines[:, depth:])

        if exchange:

            @pl.when(t == 0)
            def _():
                for g in range(groups):
                    speed_copy(g).wait()
                    for i in range(PLANES):
                        x = g * PLANES + i
                        speed[x] = jnp.where(keep, speed[x], speed_in[x])

        for row in (0, cells_y - PAD):
            advance_some(0, cells_x, row, PAD)

        @pl.when(t < iters - 1)
        def _():
            send_y(late)

        for g in sorted({0, groups - 1}):
            advance_some(g * PLANES, PLANES, PAD, cells_y - 2 * PAD)

        @pl.when(t < iters - 1)
        def _():
            send_x(late)

        for g in range(1, groups - 1):
            advance_some(g * PLANES, PLANES, PAD, cells_y - 2 * PAD)

        @pl.when(t == iters - 1)
        def _():
            result.start()

        pair = max(1, 128 // cells_y)
        wide = pair * cells_y
        for p in range(cells_x // pair):
            block = field[late, pl.ds(HALO + p * pair, pair), inner_y]
            turned = block.reshape(wide, depth).T
            for part, piece in enumerate(parts(turned)):
                lhs[part * depth : (part + 1) * depth, p * wide : (p + 1) * wide] = piece
        zs = lax.broadcasted_iota(jnp.int32, (depth, CHUNK), 0)
        for c in range(nrec // CHUNK):
            got = jnp.dot(lhs[...], hot[c], preferred_element_type=jnp.float32)
            picked = got[:depth]
            for part in range(1, PARTS):
                picked = picked + got[part * depth : (part + 1) * depth]
            cols = pl.ds(c * CHUNK, CHUNK)
            gap = picked - obs_ref[pl.ds(t, 1), cols]
            part = jnp.where(zs == rec_z[:, cols], gap * gap, 0.0)
            part = part.reshape(depth // 8, 8, CHUNK).sum(axis=0)
            acc[...] += part[:, :128] + part[:, 128:]
        return 0

    lax.fori_loop(0, iters, step, 0)

    copies = []
    for d in range(1, len(peers)):
        copy = pltpu.make_async_remote_copy(
            src_ref=acc,
            dst_ref=red.at[d],
            send_sem=red_send.at[d],
            recv_sem=red_recv.at[d],
            device_id=peers[d],
            device_id_type=MESH,
        )
        copy.start()
        copies.append(copy)
    total = acc[...]
    for d, copy in enumerate(copies, 1):
        copy.wait()
        total = total + red[d]
    result.wait()
    share = jnp.sum(total, axis=(0, 1), keepdims=True) * (1.0 / (iters * nrec))
    misfit_ref[...] = jnp.broadcast_to(share, misfit_ref.shape)


def local(
    sizes,
    velocity,
    direction,
    wave_prev,
    wave_now,
    winner,
    step_lengths,
    src_cell,
    wavelet,
    rec_cells,
    observed,
):
    trials, tiles_x, tiles_y = sizes
    cells_x, cells_y, depth = velocity.shape[1:]
    iters, nrec = observed.shape
    if trials != 2:
        root = winner[0] % trials
        velocity = from_root(velocity, "trial", root)
        direction = from_root(direction, "trial", root)
    vmem = pl.BlockSpec(memory_space=pltpu.VMEM)
    smem = pl.BlockSpec(memory_space=pltpu.SMEM)
    block = (cells_x, cells_y, depth)
    faces = (2, 2, HALO, cells_x, depth)
    tiles = tiles_x * tiles_y
    groups = cells_x // PLANES
    whole = pl.BlockSpec(memory_space=pltpu.HBM)
    out, misfit = pl.pallas_call(
        functools.partial(kernel, sizes),
        out_shape=(
            jax.ShapeDtypeStruct((1,) + block, jnp.float32),
            jax.ShapeDtypeStruct((1, 128), jnp.float32),
        ),
        in_specs=[whole] * 4 + [smem] * 4 + [whole] * 2,
        out_specs=(whole, vmem),
        scratch_shapes=[
            pltpu.VMEM((2, cells_x + 2 * HALO, cells_y + 2 * PAD, depth), jnp.float32),
            pltpu.VMEM((1, nrec), jnp.int32),
            pltpu.VMEM(block, jnp.float32),
            pltpu.VMEM(block, jnp.float32),
            pltpu.VMEM(block, jnp.float32),
            pltpu.VMEM(faces, jnp.float32),
            pltpu.VMEM(faces, jnp.float32),
            pltpu.VMEM((nrec // CHUNK, cells_x * cells_y, CHUNK), jnp.bfloat16),
            pltpu.VMEM((PARTS * depth, cells_x * cells_y), jnp.bfloat16),
            pltpu.VMEM((8, 128), jnp.float32),
            pltpu.VMEM((tiles, 8, 128), jnp.float32),
            pltpu.SemaphoreType.DMA((2, 2)),
            pltpu.SemaphoreType.DMA((2, 2)),
            pltpu.SemaphoreType.DMA((2, 2)),
            pltpu.SemaphoreType.DMA((2, 2)),
            pltpu.SemaphoreType.DMA((groups,)),
            pltpu.SemaphoreType.DMA((groups,)),
            pltpu.SemaphoreType.DMA((tiles,)),
            pltpu.SemaphoreType.DMA((tiles,)),
            pltpu.VMEM(block, jnp.float32),
            pltpu.VMEM(block, jnp.float32),
            pltpu.SemaphoreType.DMA((2, groups)),
            pltpu.SemaphoreType.DMA((2,)),
            pltpu.SemaphoreType.DMA,
            pltpu.VMEM((1, nrec), jnp.int32),
            pltpu.VMEM((iters, nrec), jnp.float32),
            pltpu.VMEM((PARTS * depth, 2 * depth), jnp.bfloat16),
            pltpu.SemaphoreType.DMA((2,)),
        ],
        compiler_params=pltpu.CompilerParams(
            collective_id=0, has_side_effects=True, vmem_limit_bytes=62 * 1024 * 1024
        ),
    )(
        velocity,
        direction,
        wave_prev,
        wave_now,
        winner,
        step_lengths,
        src_cell,
        wavelet,
        rec_cells.reshape(1, nrec),
        observed,
    )
    return out, misfit[0, :1]


def solution(mesh):
    sizes = tuple(mesh.shape[axis] for axis in ("trial", "tx", "ty"))
    spread = P("trial", "tx", "ty", None)
    return jax.shard_map(
        functools.partial(local, sizes),
        mesh=mesh,
        in_specs=(spread,) * 4 + (P(),) * 6,
        out_specs=(spread, P("trial")),
        check_vma=False,
    )
```
